32 devices in a mesh: by: 4 (over y, core), bz: 8 (over z, x).
Axes of the slice: x: 2, y: 2, z: 4, core: 2. Of those that a mesh axis runs over, the one named last changes fastest.
Arguments:
- fields: float32 [8, 64, 256, 512], P(None, 'by', 'bz'), may hold values from -400 to 400
- conductance: float32 [64, 256, 512], P('by', 'bz'), may hold values from 0.05 to 1
Outputs:
- basis: float32 [8, 64, 256, 512], P(None, 'by', 'bz')
- factor: float32 [512, 512], replicated
The draws below stay inside these ranges and needn't reach their ends.
All inputs are finite; a program needn't handle non-finite values.
Results may differ from the reference program's by a relative error of at most 0.0003.
Values sent between devices are 32-bit elements; how exact they have to be, the bound alone decides.
A program may use at most 320 MiB of HBM per device.

```python
import math
import jax
import jax.numpy as jnp
from jax import lax

X = 512
F = 8
NY = 64
NZ = 256


def draw_fields(key, part):
    key = jax.random.fold_in(key, 11)
    key_base, key_rows, key_cols = jax.random.split(key, 3)
    row_scale = jnp.exp(jax.random.uniform(key_rows, (F, NY, NZ, 1), minval=0.0, maxval=math.log(10.0)))
    col_scale = jnp.exp(jax.random.uniform(key_cols, (1, 1, 1, X), minval=0.0, maxval=math.log(10.0)))
    value = jnp.clip(jax.random.normal(key_base, (F, NY, NZ, X)), -4.0, 4.0) * row_scale * col_scale
    return value.astype(jnp.float32)


def level_of(stream_key, dims, cuts, low, high):
    loudness, own = 1.0, jax.random.fold_in(stream_key, 6)
    for dim, blocks in cuts:
        draws = jnp.exp(jax.random.uniform(jax.random.fold_in(own, dim), (blocks,), jnp.float32, low / len(cuts), high / len(cuts)))
        loudness = loudness * jnp.repeat(draws, dims[dim] // blocks).reshape([-1 if axis == dim else 1 for axis in range(len(dims))])
    return loudness


def setup_inputs(seed: int = 0) -> dict:
    seeds = jax.random.split(jax.random.key(seed), 3)
    return {
        "fields": draw_fields(jax.random.fold_in(seeds[2], 71), 0),
        "conductance": jnp.clip(jnp.exp(math.log(1.0) - 2.9957323 * jax.random.uniform(seeds[1], (NY, NZ, X), jnp.float32) ** level_of(seeds[1], (NY, NZ, X), ((0, 4), (1, 8)), -0.2, 0.2)), 0.05, 1.0),
    }


def relax(field, cond):
    padded = jnp.pad(field, 1)
    padk = jnp.pad(cond, 1)
    centre = field
    total = jnp.zeros_like(field)
    shapes = [(2, 1, 1), (0, 1, 1), (1, 2, 1), (1, 0, 1), (1, 1, 2), (1, 1, 0)]
    for start in shapes:
        nb = lax.slice(padded, start, (start[0] + field.shape[0], start[1] + field.shape[1], start[2] + field.shape[2]))
        kn = lax.slice(padk, start, (start[0] + field.shape[0], start[1] + field.shape[1], start[2] + field.shape[2]))
        total = total + jnp.sqrt(cond * kn) * (nb - centre)
    return centre + 0.125 * total

def reference(fields, conductance):

    def per_field(gram, field):
        once = relax(field, conductance)
        twice = relax(once, conductance)
        rows = twice.reshape(-1, twice.shape[-1])
        gram = gram + lax.dot_general(rows.astype(jnp.float32), rows.astype(jnp.float32), (((0,), (0,)), ((), ())), precision=lax.Precision.HIGHEST, preferred_element_type=jnp.float32)
        return (gram, twice)
    gram, relaxed = lax.scan(per_field, jnp.zeros((X, X), jnp.float32), fields)
    gram = gram / jnp.float32(F * NY * NZ)
    factor = jnp.linalg.cholesky(gram).T
    inverse = jax.scipy.linalg.solve_triangular(factor, jnp.eye(X, dtype=jnp.float32), lower=False)

    def project(field):
        rows = field.reshape(-1, X)
        return jnp.dot(rows.astype(jnp.float32), inverse.astype(jnp.float32), precision=lax.Precision.HIGHEST, preferred_element_type=jnp.float32).reshape(field.shape)
    basis = lax.map(project, relaxed)
    return (basis, factor)
```

```python
import functools

import jax
import jax.numpy as jnp
from jax import lax
from jax.experimental import pallas as pl
from jax.experimental.pallas import tpu as pltpu
from jax.sharding import PartitionSpec as P

VMEM_LIMIT = 58 * 1024 * 1024
HIGHEST = lax.Precision.HIGHEST
HIGH = lax.Precision.HIGH
STEP = 128


def shift_faces(cells, axis):
    count = lax.axis_size(axis)
    head, tail = cells
    below = lax.ppermute(tail, axis, [(i, i + 1) for i in range(count - 1)])
    above = lax.ppermute(head, axis, [(i + 1, i) for i in range(count - 1)])
    return below, above


def relax_kernel(with_faces, u_ref, k_ref, yb_ref, ya_ref, zb_ref, za_ref, kyb_ref, kya_ref, kzb_ref, kza_ref, *rest):
    if with_faces:
        out_ref, ylo_ref, yhi_ref, zlo_ref, zhi_ref, ext, root = rest
    else:
        out_ref, ext, root = rest
    nf, ny, nz, nx = u_ref.shape
    top = 8 + nz

    def fill_root(y, carry):
        root[y + 1, pl.ds(8, nz), :] = jnp.sqrt(k_ref[y])
        return carry

    lax.fori_loop(0, ny, fill_root, 0)
    root[0, pl.ds(8, nz), :] = jnp.sqrt(kyb_ref[...])
    root[ny + 1, pl.ds(8, nz), :] = jnp.sqrt(kya_ref[...])
    root[pl.ds(1, ny), 7:8, :] = jnp.sqrt(kzb_ref[...])[:, None, :]
    root[pl.ds(1, ny), top : top + 1, :] = jnp.sqrt(kza_ref[...])[:, None, :]

    def fill(f, carry):
        def fill_y(y, c):
            ext[f, y + 1, pl.ds(8, nz), :] = u_ref[f, y]
            return c

        lax.fori_loop(0, ny, fill_y, 0)
        ext[f, 0, pl.ds(8, nz), :] = yb_ref[f]
        ext[f, ny + 1, pl.ds(8, nz), :] = ya_ref[f]
        ext[f, pl.ds(1, ny), 7:8, :] = zb_ref[f][:, None, :]
        ext[f, pl.ds(1, ny), top : top + 1, :] = za_ref[f][:, None, :]
        return carry

    lax.fori_loop(0, nf, fill, 0)

    lane = lax.broadcasted_iota(jnp.int32, (8, nx), 1)

    def plane(y, carry):
        for z in range(0, nz, 8):
            centre = 0.125 * root[y + 1, pl.ds(8 + z, 8), :]
            plain = root[y + 1, pl.ds(8 + z, 8), :]
            wyp = centre * root[y + 2, pl.ds(8 + z, 8), :]
            wym = centre * root[y, pl.ds(8 + z, 8), :]
            wzp = centre * root[y + 1, pl.ds(9 + z, 8), :]
            wzm = centre * root[y + 1, pl.ds(7 + z, 8), :]
            wxp = jnp.where(lane == nx - 1, 0.0, centre * pltpu.roll(plain, nx - 1, 1))
            wxm = jnp.where(lane == 0, 0.0, centre * pltpu.roll(plain, 1, 1))
            keep = 1.0 - (((wyp + wym) + (wzp + wzm)) + (wxp + wxm))
            for f in range(nf):
                mid = ext[f, y + 1, pl.ds(8 + z, 8), :]
                near = wyp * ext[f, y + 2, pl.ds(8 + z, 8), :] + wym * ext[f, y, pl.ds(8 + z, 8), :]
                side = wzp * ext[f, y + 1, pl.ds(9 + z, 8), :] + wzm * ext[f, y + 1, pl.ds(7 + z, 8), :]
                along = wxp * pltpu.roll(mid, nx - 1, 1) + wxm * pltpu.roll(mid, 1, 1)
                out_ref[f, y, pl.ds(z, 8), :] = (keep * mid + near) + (side + along)
        return carry

    lax.fori_loop(0, ny, plane, 0)
    if with_faces:
        for f in range(nf):
            ylo_ref[f] = out_ref[f, 0]
            yhi_ref[f] = out_ref[f, ny - 1]
            zlo_ref[f] = out_ref[f, :, 0, :]
            zhi_ref[f] = out_ref[f, :, nz - 1, :]


def relax_call(u, k, faces, kfaces, with_faces):
    nf, ny, nz, nx = u.shape
    full = jax.ShapeDtypeStruct(u.shape, jnp.float32)
    yface = jax.ShapeDtypeStruct((nf, nz, nx), jnp.float32)
    zface = jax.ShapeDtypeStruct((nf, ny, nx), jnp.float32)
    outs = [full] + ([yface, yface, zface, zface] if with_faces else [])
    return pl.pallas_call(
        functools.partial(relax_kernel, with_faces),
        out_shape=outs,
        in_specs=[pl.BlockSpec(memory_space=pltpu.VMEM)] * 10,
        out_specs=[pl.BlockSpec(memory_space=pltpu.VMEM)] * len(outs),
        scratch_shapes=[
            pltpu.VMEM((nf, ny + 2, nz + 16, nx), jnp.float32),
            pltpu.VMEM((ny + 2, nz + 16, nx), jnp.float32),
        ],
        compiler_params=pltpu.CompilerParams(vmem_limit_bytes=VMEM_LIMIT),
        name="relax",
    )(u, k, *faces, *kfaces)


def eliminate(block):
    size = block.shape[0]
    groups = size // 8
    row8 = lax.broadcasted_iota(jnp.int32, (8, size), 0)
    lane8 = lax.broadcasted_iota(jnp.int32, (8, size), 1)
    work = [block[8 * g : 8 * g + 8] for g in range(groups)]
    side = [jnp.where(row8 + 8 * g == lane8, 1.0, 0.0) for g in range(groups)]
    for j in range(size):
        g, r = divmod(j, 8)
        spread = jnp.broadcast_to(work[g][:, j : j + 1], (8, size))
        inv = 1.0 / jnp.broadcast_to(spread[r : r + 1], (8, size))
        row = jnp.broadcast_to(work[g][r : r + 1], (8, size)) * inv
        arow = jnp.broadcast_to(side[g][r : r + 1], (8, size)) * inv
        for q in range(g, groups):
            if q == g:
                if r == 7:
                    continue
                mult = jnp.where(row8 > r, spread, 0.0)
            else:
                mult = jnp.broadcast_to(work[q][:, j : j + 1], (8, size))
            work[q] = work[q] - mult * row
            side[q] = side[q] - mult * arow
    return jnp.concatenate(work, axis=0), jnp.concatenate(side, axis=0)


def factor_kernel(gram_ref, factor_ref, inv_ref, work, side):
    n = gram_ref.shape[0]
    step = min(n, STEP)
    count = n // step
    big = (((1,), (0,)), ((), ()))
    tall = (((0,), (0,)), ((), ()))
    rows = lax.broadcasted_iota(jnp.int32, (step, step), 0)
    cols = lax.broadcasted_iota(jnp.int32, (step, step), 1)
    col_n = lax.broadcasted_iota(jnp.int32, (step, n), 1)
    row_n = lax.broadcasted_iota(jnp.int32, (step, n), 0)
    work[...] = gram_ref[...]
    side[...] = jnp.zeros_like(side)

    def block_step(k, carry):
        lo = pl.multiple_of(k * step, step)
        here = pl.ds(lo, step)
        upper, lower = eliminate(work[here, here])
        pivot = jnp.sum(jnp.where(rows == cols, upper, 0.0), axis=1, keepdims=True)
        scale = 1.0 / jnp.sqrt(pivot)
        linv = lower * scale
        solved = lax.dot_general(linv, work[here, :], big, precision=HIGHEST, preferred_element_type=jnp.float32)
        factor_ref[here, :] = jnp.where(col_n >= row_n + lo, solved, 0.0)
        factor_ref[here, here] = jnp.where(cols >= rows, upper * scale, 0.0)
        left = side[here, :]
        left = lax.dot_general(linv, left, big, precision=HIGHEST, preferred_element_type=jnp.float32)
        inv_ref[here, :] = left
        inv_ref[here, here] = linv

        def trail(i, c):
            there = pl.ds(pl.multiple_of(i * step, step), step)
            mult = factor_ref[here, there]
            work[there, :] -= lax.dot_general(mult, factor_ref[here, :], tall, precision=HIGHEST, preferred_element_type=jnp.float32)
            side[there, :] -= lax.dot_general(mult, inv_ref[here, :], tall, precision=HIGHEST, preferred_element_type=jnp.float32)
            return c

        lax.fori_loop(k + 1, count, trail, 0)
        return carry

    lax.fori_loop(0, count, block_step, 0)


def factor_call(gram):
    shape = jax.ShapeDtypeStruct(gram.shape, jnp.float32)
    return pl.pallas_call(
        factor_kernel,
        out_shape=[shape, shape],
        in_specs=[pl.BlockSpec(memory_space=pltpu.VMEM)],
        out_specs=[pl.BlockSpec(memory_space=pltpu.VMEM)] * 2,
        scratch_shapes=[pltpu.VMEM(gram.shape, jnp.float32)] * 2,
        compiler_params=pltpu.CompilerParams(vmem_limit_bytes=VMEM_LIMIT),
        name="factor",
    )(gram)


def on_device(fields, conductance):
    nf, ny, nz, nx = fields.shape
    total_rows = nf * ny * lax.axis_size("by") * nz * lax.axis_size("bz")
    stacked = lambda f, k: jnp.concatenate([f, k[None]], axis=0)
    yfaces = shift_faces(
        (stacked(fields[:, 0], conductance[0]), stacked(fields[:, ny - 1], conductance[ny - 1])), "by"
    )
    zfaces = shift_faces(
        (stacked(fields[:, :, 0], conductance[:, 0]), stacked(fields[:, :, nz - 1], conductance[:, nz - 1])), "bz"
    )
    faces = [a[:nf] for a in (*yfaces, *zfaces)]
    kfaces = [a[nf] for a in (*yfaces, *zfaces)]
    once, ylo, yhi, zlo, zhi = relax_call(fields, conductance, faces, kfaces, True)
    again = (*shift_faces((ylo, yhi), "by"), *shift_faces((zlo, zhi), "bz"))
    relaxed = relax_call(once, conductance, again, kfaces, False)[0]
    rows = relaxed.reshape(-1, nx)
    gram = lax.dot_general(
        rows, rows, (((0,), (0,)), ((), ())), precision=HIGH, preferred_element_type=jnp.float32
    )
    gram = lax.psum(gram / jnp.float32(total_rows), ("by", "bz"))
    factor, linv = factor_call(gram)
    basis = lax.dot_general(
        rows, linv, (((1,), (1,)), ((), ())), precision=HIGH, preferred_element_type=jnp.float32
    )
    return (basis.reshape(relaxed.shape), factor)


def solution(mesh):
    return jax.shard_map(
        on_device,
        mesh=mesh,
        in_specs=(P(None, "by", "bz", None), P("by", "bz", None)),
        out_specs=(P(None, "by", "bz", None), P()),
        check_vma=False,
    )
```

```python
import functools

import jax
import jax.numpy as jnp
from jax import lax
from jax.experimental import pallas as pl
from jax.experimental.pallas import tpu as pltpu
from jax.sharding import PartitionSpec as P

VMEM_LIMIT = 58 * 1024 * 1024
HIGHEST = lax.Precision.HIGHEST
HIGH = lax.Precision.HIGH
STEP = 128


def shift_faces(cells, axis):
    count = lax.axis_size(axis)
    head, tail = cells
    below = lax.ppermute(tail, axis, [(i, i + 1) for i in range(count - 1)])
    above = lax.ppermute(head, axis, [(i + 1, i) for i in range(count - 1)])
    return below, above


def upper_blocks(n):
    count = n // STEP
    return [(i, j) for i in range(count) for j in range(i, count)]


def relax_kernel(with_faces, total_rows, u_ref, k_ref, yb_ref, ya_ref, zb_ref, za_ref, kyb_ref, kya_ref, kzb_ref, kza_ref, *rest):
    if with_faces:
        out_ref, ylo_ref, yhi_ref, zlo_ref, zhi_ref, ext, root = rest
    else:
        out_ref, gram_ref, ext, root, head, cross = rest
    nf, ny, nz, nx = u_ref.shape
    top = 8 + nz

    def fill_root(y, carry):
        root[y + 1, pl.ds(8, nz), :] = jnp.sqrt(k_ref[y])
        return carry

    lax.fori_loop(0, ny, fill_root, 0)
    root[0, pl.ds(8, nz), :] = jnp.sqrt(kyb_ref[...])
    root[ny + 1, pl.ds(8, nz), :] = jnp.sqrt(kya_ref[...])
    root[pl.ds(1, ny), 7:8, :] = jnp.sqrt(kzb_ref[...])[:, None, :]
    root[pl.ds(1, ny), top : top + 1, :] = jnp.sqrt(kza_ref[...])[:, None, :]

    def fill(f, carry):
        def fill_y(y, c):
            ext[f, y + 1, pl.ds(8, nz), :] = u_ref[f, y]
            return c

        lax.fori_loop(0, ny, fill_y, 0)
        ext[f, 0, pl.ds(8, nz), :] = yb_ref[f]
        ext[f, ny + 1, pl.ds(8, nz), :] = ya_ref[f]
        ext[f, pl.ds(1, ny), 7:8, :] = zb_ref[f][:, None, :]
        ext[f, pl.ds(1, ny), top : top + 1, :] = za_ref[f][:, None, :]
        return carry

    lax.fori_loop(0, nf, fill, 0)

    lane = lax.broadcasted_iota(jnp.int32, (8, nx), 1)

    def plane(y, carry):
        for z in range(0, nz, 8):
            centre = 0.125 * root[y + 1, pl.ds(8 + z, 8), :]
            plain = root[y + 1, pl.ds(8 + z, 8), :]
            wyp = centre * root[y + 2, pl.ds(8 + z, 8), :]
            wym = centre * root[y, pl.ds(8 + z, 8), :]
            wzp = centre * root[y + 1, pl.ds(9 + z, 8), :]
            wzm = centre * root[y + 1, pl.ds(7 + z, 8), :]
            wxp = jnp.where(lane == nx - 1, 0.0, centre * pltpu.roll(plain, nx - 1, 1))
            wxm = jnp.where(lane == 0, 0.0, centre * pltpu.roll(plain, 1, 1))
            keep = 1.0 - (((wyp + wym) + (wzp + wzm)) + (wxp + wxm))
            for f in range(nf):
                mid = ext[f, y + 1, pl.ds(8 + z, 8), :]
                near = wyp * ext[f, y + 2, pl.ds(8 + z, 8), :] + wym * ext[f, y, pl.ds(8 + z, 8), :]
                side = wzp * ext[f, y + 1, pl.ds(9 + z, 8), :] + wzm * ext[f, y + 1, pl.ds(7 + z, 8), :]
                along = wxp * pltpu.roll(mid, nx - 1, 1) + wxm * pltpu.roll(mid, 1, 1)
                out_ref[f, y, pl.ds(z, 8), :] = (keep * mid + near) + (side + along)
        return carry

    lax.fori_loop(0, ny, plane, 0)
    if with_faces:
        for f in range(nf):
            ylo_ref[f] = out_ref[f, 0]
            yhi_ref[f] = out_ref[f, ny - 1]
            zlo_ref[f] = out_ref[f, :, 0, :]
            zhi_ref[f] = out_ref[f, :, nz - 1, :]
    else:
        pack_gram(total_rows, out_ref, gram_ref, head, cross)


def pack_gram(total_rows, rows_ref, gram_ref, head, cross):
    nf, ny, nz, nx = rows_ref.shape
    half = nx // 2
    tall = (((0,), (0,)), ((), ()))
    head[...] = jnp.zeros_like(head)
    cross[...] = jnp.zeros_like(cross)

    def add(f, carry):
        x = rows_ref[f].reshape(ny * nz, nx)
        hi = x.astype(jnp.bfloat16)
        lo = (x - hi.astype(jnp.float32)).astype(jnp.bfloat16)
        for c in range(2):
            cols = slice(c * half, (c + 1) * half)
            left = hi[:, cols]
            cross[cols, :] += lax.dot_general(left, lo, tall, preferred_element_type=jnp.float32)
            head[cols, c * half :] += lax.dot_general(left, hi[:, c * half :], tall, preferred_element_type=jnp.float32)
        return carry

    lax.fori_loop(0, nf, add, 0)
    for b, (i, j) in enumerate(upper_blocks(nx)):
        ri, rj = slice(i * STEP, (i + 1) * STEP), slice(j * STEP, (j + 1) * STEP)
        total = head[ri, rj] + (cross[ri, rj] + cross[rj, ri].T)
        gram_ref[b * STEP : (b + 1) * STEP, :] = total / jnp.float32(total_rows)


def relax_call(u, k, faces, kfaces, with_faces, total_rows=1):
    nf, ny, nz, nx = u.shape
    full = jax.ShapeDtypeStruct(u.shape, jnp.float32)
    yface = jax.ShapeDtypeStruct((nf, nz, nx), jnp.float32)
    zface = jax.ShapeDtypeStruct((nf, ny, nx), jnp.float32)
    packed = jax.ShapeDtypeStruct((len(upper_blocks(nx)) * STEP, STEP), jnp.float32)
    outs = [full] + ([yface, yface, zface, zface] if with_faces else [packed])
    return pl.pallas_call(
        functools.partial(relax_kernel, with_faces, total_rows),
        out_shape=outs,
        in_specs=[pl.BlockSpec(memory_space=pltpu.VMEM)] * 10,
        out_specs=[pl.BlockSpec(memory_space=pltpu.VMEM)] * len(outs),
        scratch_shapes=[
            pltpu.VMEM((nf, ny + 2, nz + 16, nx), jnp.float32),
            pltpu.VMEM((ny + 2, nz + 16, nx), jnp.float32),
        ]
        + ([] if with_faces else [pltpu.VMEM((nx, nx), jnp.float32)] * 2),
        compiler_params=pltpu.CompilerParams(vmem_limit_bytes=VMEM_LIMIT),
        name="relax",
    )(u, k, *faces, *kfaces)


def tree_sum(terms):
    while len(terms) > 1:
        terms = [a + b for a, b in zip(terms[::2], terms[1::2])]
    return terms[0]


def eliminate(block):
    size = block.shape[0]
    groups = size // 8
    row8 = lax.broadcasted_iota(jnp.int32, (8, size), 0)
    lane8 = lax.broadcasted_iota(jnp.int32, (8, size), 1)
    work = [block[8 * g : 8 * g + 8] for g in range(groups)]
    side = [jnp.where(row8 + 8 * g == lane8, 1.0, 0.0) for g in range(groups)]
    for p in range(groups):
        rows, arows = work[p], side[p]
        spread = [jnp.broadcast_to(rows[:, 8 * p + m : 8 * p + m + 1], (8, size)) for m in range(8)]
        unit, aunit = [], []
        for m in range(8):
            inv = 1.0 / jnp.broadcast_to(spread[m][m : m + 1], (8, size))
            unit.append(jnp.broadcast_to(rows[m : m + 1], (8, size)) * inv)
            aunit.append(jnp.broadcast_to(arows[m : m + 1], (8, size)) * inv)
            if m < 7:
                mult = jnp.where(row8 > m, spread[m], 0.0)
                rows = rows - mult * unit[m]
                arows = arows - mult * aunit[m]
                for t in range(m + 1, 8):
                    spread[t] = spread[t] - mult * (jnp.broadcast_to(spread[t][m : m + 1], (8, size)) * inv)
        work[p], side[p] = rows, arows
        if p + 1 < groups:
            tall = rows.T
            for q in range(p + 1, groups):
                mults = [jnp.broadcast_to(tall[8 * q : 8 * q + 8, m : m + 1], (8, size)) for m in range(8)]
                work[q] = work[q] - tree_sum([a * b for a, b in zip(mults, unit)])
                side[q] = side[q] - tree_sum([a * b for a, b in zip(mults, aunit)])
    return jnp.concatenate(work, axis=0), jnp.concatenate(side, axis=0)


def factor_kernel(gram_ref, factor_ref, inv_ref, work, side):
    n = factor_ref.shape[0]
    step = STEP
    count = n // step
    big = (((1,), (0,)), ((), ()))
    tall = (((0,), (0,)), ((), ()))
    rows = lax.broadcasted_iota(jnp.int32, (step, step), 0)
    cols = lax.broadcasted_iota(jnp.int32, (step, step), 1)
    col_n = lax.broadcasted_iota(jnp.int32, (step, n), 1)
    row_n = lax.broadcasted_iota(jnp.int32, (step, n), 0)
    work[...] = jnp.zeros_like(work)
    for b, (i, j) in enumerate(upper_blocks(n)):
        work[i * step : (i + 1) * step, j * step : (j + 1) * step] = gram_ref[b * step : (b + 1) * step, :]
    side[...] = jnp.zeros_like(side)

    def block_step(k, carry):
        lo = pl.multiple_of(k * step, step)
        here = pl.ds(lo, step)
        upper, lower = eliminate(work[here, here])
        pivot = jnp.sum(jnp.where(rows == cols, upper, 0.0), axis=1, keepdims=True)
        scale = 1.0 / jnp.sqrt(pivot)
        linv = lower * scale
        solved = lax.dot_general(linv, work[here, :], big, precision=HIGHEST, preferred_element_type=jnp.float32)
        factor_ref[here, :] = jnp.where(col_n >= row_n + lo, solved, 0.0)
        factor_ref[here, here] = jnp.where(cols >= rows, upper * scale, 0.0)
        left = side[here, :]
        left = lax.dot_general(linv, left, big, precision=HIGHEST, preferred_element_type=jnp.float32)
        inv_ref[here, :] = left
        inv_ref[here, here] = linv

        def trail(i, c):
            there = pl.ds(pl.multiple_of(i * step, step), step)
            mult = factor_ref[here, there]
            work[there, :] -= lax.dot_general(mult, factor_ref[here, :], tall, precision=HIGHEST, preferred_element_type=jnp.float32)
            side[there, :] -= lax.dot_general(mult, inv_ref[here, :], tall, precision=HIGHEST, preferred_element_type=jnp.float32)
            return c

        lax.fori_loop(k + 1, count, trail, 0)
        return carry

    lax.fori_loop(0, count, block_step, 0)


def factor_call(gram, n):
    shape = jax.ShapeDtypeStruct((n, n), jnp.float32)
    return pl.pallas_call(
        factor_kernel,
        out_shape=[shape, shape],
        in_specs=[pl.BlockSpec(memory_space=pltpu.VMEM)],
        out_specs=[pl.BlockSpec(memory_space=pltpu.VMEM)] * 2,
        scratch_shapes=[pltpu.VMEM((n, n), jnp.float32)] * 2,
        compiler_params=pltpu.CompilerParams(vmem_limit_bytes=VMEM_LIMIT),
        name="factor",
    )(gram)


FAST = 2


def sum_kernel(nby, nbz, in_ref, out_ref, land_a, land_b, part, send_a, recv_a, send_b, recv_b, send_c, recv_c, send_d, recv_d):
    na, nb = nby * FAST, nbz // FAST
    rows_a = in_ref.shape[0] // na
    rows_b = rows_a // nb
    by, bz = lax.axis_index("by"), lax.axis_index("bz")
    a = by * FAST + bz % FAST
    z = bz // FAST

    def plane_peer(d):
        t = (a + d) % na
        return t, (t // FAST, z * FAST + t % FAST)

    def line_peer(d):
        t = (z + d) % nb
        return t, (by, t * FAST + bz % FAST)

    barrier = pltpu.get_barrier_semaphore()
    for d in range(1, na):
        pl.semaphore_signal(barrier, inc=1, device_id=plane_peer(d)[1], device_id_type=pl.DeviceIdType.MESH)
    for d in range(1, nb):
        pl.semaphore_signal(barrier, inc=1, device_id=line_peer(d)[1], device_id_type=pl.DeviceIdType.MESH)
    pl.semaphore_wait(barrier, na + nb - 2)

    def exchange(peer, count, send, recv, source, target):
        copies = []
        for d in range(1, count):
            t, where = peer(d)
            copy = pltpu.make_async_remote_copy(
                src_ref=source(t),
                dst_ref=target(d),
                send_sem=send.at[d - 1],
                recv_sem=recv.at[d - 1],
                device_id=where,
                device_id_type=pl.DeviceIdType.MESH,
            )
            copy.start()
            copies.append(copy)
        for copy in copies:
            copy.wait()

    def rows_at(base, size):
        return pl.ds(pl.multiple_of(base, 8), size)

    exchange(plane_peer, na, send_a, recv_a, lambda t: in_ref.at[rows_at(t * rows_a, rows_a)], lambda d: land_a.at[d - 1])
    part[...] = in_ref[rows_at(a * rows_a, rows_a), :] + tree_any([land_a[d] for d in range(na - 1)])
    exchange(line_peer, nb, send_b, recv_b, lambda t: part.at[rows_at(t * rows_b, rows_b)], lambda d: land_b.at[d - 1])
    mine = rows_at(a * rows_a + z * rows_b, rows_b)
    out_ref[mine, :] = part[rows_at(z * rows_b, rows_b), :] + tree_any([land_b[d] for d in range(nb - 1)])
    exchange(line_peer, nb, send_c, recv_c, lambda t: out_ref.at[mine], lambda d: out_ref.at[mine])
    ours = rows_at(a * rows_a, rows_a)
    exchange(plane_peer, na, send_d, recv_d, lambda t: out_ref.at[ours], lambda d: out_ref.at[ours])


def tree_any(terms):
    total = terms[0]
    for term in terms[1:]:
        total = total + term
    return total


def sum_call(packed):
    nby, nbz = lax.axis_size("by"), lax.axis_size("bz")
    na, nb = nby * FAST, nbz // FAST
    rows, cols = packed.shape
    if nbz % FAST or nb < 2 or rows % (8 * na * nb):
        return lax.psum(packed, ("by", "bz"))
    rows_a = rows // na
    rows_b = rows_a // nb
    sems = [pltpu.SemaphoreType.DMA((c - 1,)) for c in (na, na, nb, nb, nb, nb, na, na)]
    return pl.pallas_call(
        functools.partial(sum_kernel, nby, nbz),
        out_shape=jax.ShapeDtypeStruct(packed.shape, jnp.float32),
        in_specs=[pl.BlockSpec(memory_space=pltpu.VMEM)],
        out_specs=pl.BlockSpec(memory_space=pltpu.VMEM),
        scratch_shapes=[
            pltpu.VMEM((na - 1, rows_a, cols), jnp.float32),
            pltpu.VMEM((nb - 1, rows_b, cols), jnp.float32),
            pltpu.VMEM((rows_a, cols), jnp.float32),
            *sems,
        ],
        compiler_params=pltpu.CompilerParams(collective_id=0, has_side_effects=True, vmem_limit_bytes=VMEM_LIMIT),
        name="sum_all",
    )(packed)


def on_device(fields, conductance):
    nf, ny, nz, nx = fields.shape
    total_rows = nf * ny * lax.axis_size("by") * nz * lax.axis_size("bz")
    stacked = lambda f, k: jnp.concatenate([f, k[None]], axis=0)
    yfaces = shift_faces(
        (stacked(fields[:, 0], conductance[0]), stacked(fields[:, ny - 1], conductance[ny - 1])), "by"
    )
    zfaces = shift_faces(
        (stacked(fields[:, :, 0], conductance[:, 0]), stacked(fields[:, :, nz - 1], conductance[:, nz - 1])), "bz"
    )
    faces = [a[:nf] for a in (*yfaces, *zfaces)]
    kfaces = [a[nf] for a in (*yfaces, *zfaces)]
    once, ylo, yhi, zlo, zhi = relax_call(fields, conductance, faces, kfaces, True)
    again = (*shift_faces((ylo, yhi), "by"), *shift_faces((zlo, zhi), "bz"))
    relaxed, packed = relax_call(once, conductance, again, kfaces, False, total_rows)
    rows = relaxed.reshape(-1, nx)
    factor, linv = factor_call(sum_call(packed), nx)
    basis = lax.dot_general(
        rows, linv, (((1,), (1,)), ((), ())), precision=HIGH, preferred_element_type=jnp.float32
    )
    return (basis.reshape(relaxed.shape), factor)


def solution(mesh):
    return jax.shard_map(
        on_device,
        mesh=mesh,
        in_specs=(P(None, "by", "bz", None), P("by", "bz", None)),
        out_specs=(P(None, "by", "bz", None), P()),
        check_vma=False,
    )
```

```python
import functools

import jax
import jax.numpy as jnp
from jax import lax
from jax.experimental import pallas as pl
from jax.experimental.pallas import tpu as pltpu
from jax.sharding import PartitionSpec as P

VMEM_LIMIT = 58 * 1024 * 1024
HIGHEST = lax.Precision.HIGHEST
HIGH = lax.Precision.HIGH
STEP = 128


def upper_blocks(n):
    count = n // STEP
    return [(i, j) for i in range(count) for j in range(i, count)]


def strip(src, root, store, y, z, nf, nx, lane):
    plain = root[y + 1, pl.ds(8 + z, 8), :]
    centre = 0.125 * plain
    wyp = centre * root[y + 2, pl.ds(8 + z, 8), :]
    wym = centre * root[y, pl.ds(8 + z, 8), :]
    wzp = centre * root[y + 1, pl.ds(9 + z, 8), :]
    wzm = centre * root[y + 1, pl.ds(7 + z, 8), :]
    wxp = jnp.where(lane == nx - 1, 0.0, centre * pltpu.roll(plain, nx - 1, 1))
    wxm = jnp.where(lane == 0, 0.0, centre * pltpu.roll(plain, 1, 1))
    keep = 1.0 - (((wyp + wym) + (wzp + wzm)) + (wxp + wxm))
    for f in range(nf):
        mid = src[f, y + 1, pl.ds(8 + z, 8), :]
        near = wyp * src[f, y + 2, pl.ds(8 + z, 8), :] + wym * src[f, y, pl.ds(8 + z, 8), :]
        side = wzp * src[f, y + 1, pl.ds(9 + z, 8), :] + wzm * src[f, y + 1, pl.ds(7 + z, 8), :]
        along = wxp * pltpu.roll(mid, nx - 1, 1) + wxm * pltpu.roll(mid, 1, 1)
        store(f, y, z, (keep * mid + near) + (side + along))


def relax_kernel(nby, nbz, u_ref, k_ref, out_ref, ext, again, root, kland, zsend, zland, zsend2, zland2, load_sem, send, recv):
    nf, ny, nz, nx = u_ref.shape
    top = 8 + nz
    by, bz = lax.axis_index("by"), lax.axis_index("bz")
    has = [by > 0, by < nby - 1, bz > 0, bz < nbz - 1]
    peer = [(by - 1, bz), (by + 1, bz), (by, bz - 1), (by, bz + 1)]
    inner = pl.ds(8, nz)
    halo = [0, ny + 1]
    mesh_id = pl.DeviceIdType.MESH

    load = pltpu.make_async_copy(u_ref, ext.at[:, pl.ds(1, ny), inner, :], load_sem)
    load.start()

    def send_item(d, base, src, place):
        return pltpu.make_async_remote_copy(
            src_ref=src,
            dst_ref=place((d + 1) % 2),
            send_sem=send.at[base + d % 2],
            recv_sem=recv.at[base + (d + 1) % 2],
            device_id=peer[d],
            device_id_type=mesh_id,
        )

    def recv_item(d, base, src, place):
        return pltpu.make_async_remote_copy(
            src_ref=src,
            dst_ref=place(d % 2),
            send_sem=send.at[base + d % 2],
            recv_sem=recv.at[base + d % 2],
            device_id=peer[d],
            device_id_type=mesh_id,
        )

    def start(items):
        for d, base, src, place in items:
            @pl.when(has[d])
            def _(d=d, base=base, src=src, place=place):
                send_item(d, base, src, place).start()

    def finish(items):
        for d, base, src, place in items:
            @pl.when(has[d])
            def _(d=d, base=base, src=src, place=place):
                recv_item(d, base, src, place).wait_recv()
                send_item(d, base, src, place).wait_send()

    barrier = pltpu.get_barrier_semaphore()
    for d in range(4):
        @pl.when(has[d])
        def _(d=d):
            pl.semaphore_signal(barrier, inc=1, device_id=peer[d], device_id_type=mesh_id)
    pl.semaphore_wait(barrier, sum(jnp.where(h, 1, 0) for h in has))

    ends = [0, ny - 1]
    first_y = [(d, 0, u_ref.at[:, ends[d]], lambda s: ext.at[:, halo[s], inner, :]) for d in range(2)]
    first_k = [(d, 2, k_ref.at[ends[d]], lambda s: kland.at[s]) for d in range(2)]
    start(first_y + first_k)

    for d in range(2):
        @pl.when(jnp.logical_not(has[d]))
        def _(d=d):
            for f in range(nf):
                ext[f, halo[d], inner, :] = jnp.zeros((nz, nx), jnp.float32)
                again[f, halo[d], inner, :] = jnp.zeros((nz, nx), jnp.float32)
            kland[d] = jnp.zeros((nz, nx), jnp.float32)

        @pl.when(jnp.logical_not(has[d + 2]))
        def _(d=d):
            zland[d] = jnp.zeros(zland.shape[1:], jnp.float32)
            zland2[d] = jnp.zeros(zland2.shape[1:], jnp.float32)

    zsend[0, nf] = k_ref[:, 0, :]
    zsend[1, nf] = k_ref[:, nz - 1, :]
    load.wait()
    for f in range(nf):
        zsend[0, f] = ext[f, pl.ds(1, ny), 8, :]
        zsend[1, f] = ext[f, pl.ds(1, ny), top - 1, :]
    first_z = [(d, 4, zsend.at[d - 2], lambda s: zland.at[s]) for d in (2, 3)]
    start(first_z)

    def fill_root(y, carry):
        root[y + 1, inner, :] = jnp.sqrt(k_ref[y])
        return carry

    lax.fori_loop(0, ny, fill_root, 0)
    lane = lax.broadcasted_iota(jnp.int32, (8, nx), 1)

    def to_again(f, y, z, value):
        again[f, y + 1, pl.ds(8 + z, 8), :] = value

    def to_out(f, y, z, value):
        out_ref[f, y, pl.ds(z, 8), :] = value

    def inside(src, store):
        def body(y, carry):
            for z in range(8, nz - 8, 8):
                strip(src, root, store, y, z, nf, nx, lane)
            return carry

        lax.fori_loop(1, ny - 1, body, 0)

    def border(src, store):
        def planes(i, carry):
            for z in range(0, nz, 8):
                strip(src, root, store, i * (ny - 1), z, nf, nx, lane)
            return carry

        def strips(y, carry):
            for z in (0, nz - 8):
                strip(src, root, store, y, z, nf, nx, lane)
            return carry

        lax.fori_loop(0, 2, planes, 0)
        lax.fori_loop(1, ny - 1, strips, 0)

    inside(ext, to_again)
    finish(first_y + first_k + first_z)
    for d, row in ((0, 7), (1, top)):
        root[halo[d], inner, :] = jnp.sqrt(kland[d])
        root[pl.ds(1, ny), row : row + 1, :] = jnp.sqrt(zland[d, nf])[:, None, :]
        for f in range(nf):
            ext[f, pl.ds(1, ny), row : row + 1, :] = zland[d, f][:, None, :]
    border(ext, to_again)

    for f in range(nf):
        zsend2[0, f] = again[f, pl.ds(1, ny), 8, :]
        zsend2[1, f] = again[f, pl.ds(1, ny), top - 1, :]
    second = [(d, 6, again.at[:, ends[d] + 1, inner, :], lambda s: again.at[:, halo[s], inner, :]) for d in range(2)]
    second += [(d, 8, zsend2.at[d - 2], lambda s: zland2.at[s]) for d in (2, 3)]
    start(second)
    inside(again, to_out)
    finish(second)
    for d, row in ((0, 7), (1, top)):
        for f in range(nf):
            again[f, pl.ds(1, ny), row : row + 1, :] = zland2[d, f][:, None, :]
    border(again, to_out)


def relax_call(u, k):
    nf, ny, nz, nx = u.shape
    cells = pltpu.VMEM((nf, ny + 2, nz + 16, nx), jnp.float32)
    return pl.pallas_call(
        functools.partial(relax_kernel, lax.axis_size("by"), lax.axis_size("bz")),
        out_shape=jax.ShapeDtypeStruct(u.shape, jnp.float32),
        in_specs=[pl.BlockSpec(memory_space=pl.ANY), pl.BlockSpec(memory_space=pltpu.VMEM)],
        out_specs=pl.BlockSpec(memory_space=pltpu.VMEM),
        scratch_shapes=[
            cells,
            cells,
            pltpu.VMEM((ny + 2, nz + 16, nx), jnp.float32),
            pltpu.VMEM((2, nz, nx), jnp.float32),
            pltpu.VMEM((2, nf + 1, ny, nx), jnp.float32),
            pltpu.VMEM((2, nf + 1, ny, nx), jnp.float32),
            pltpu.VMEM((2, nf, ny, nx), jnp.float32),
            pltpu.VMEM((2, nf, ny, nx), jnp.float32),
            pltpu.SemaphoreType.DMA,
            pltpu.SemaphoreType.DMA((10,)),
            pltpu.SemaphoreType.DMA((10,)),
        ],
        compiler_params=pltpu.CompilerParams(collective_id=1, has_side_effects=True, vmem_limit_bytes=VMEM_LIMIT),
        name="relax",
    )(u, k)


def gram_kernel(total_rows, rows_ref, gram_ref, head, cross):
    nx = rows_ref.shape[1]
    half = nx // 2
    tall = (((0,), (0,)), ((), ()))
    step = pl.program_id(0)

    @pl.when(step == 0)
    def _():
        head[...] = jnp.zeros_like(head)
        cross[...] = jnp.zeros_like(cross)

    x = rows_ref[...]
    hi = x.astype(jnp.bfloat16)
    lo = (x - hi.astype(jnp.float32)).astype(jnp.bfloat16)
    for c in range(2):
        cols = slice(c * half, (c + 1) * half)
        left = hi[:, cols]
        cross[cols, :] += lax.dot_general(left, lo, tall, preferred_element_type=jnp.float32)
        head[cols, c * half :] += lax.dot_general(left, hi[:, c * half :], tall, preferred_element_type=jnp.float32)

    @pl.when(step == pl.num_programs(0) - 1)
    def _():
        for b, (i, j) in enumerate(upper_blocks(nx)):
            ri, rj = slice(i * STEP, (i + 1) * STEP), slice(j * STEP, (j + 1) * STEP)
            total = head[ri, rj] + (cross[ri, rj] + cross[rj, ri].T)
            gram_ref[b * STEP : (b + 1) * STEP, :] = total / jnp.float32(total_rows)


def gram_call(rows, total_rows, parts):
    count, nx = rows.shape
    packed = (len(upper_blocks(nx)) * STEP, STEP)
    return pl.pallas_call(
        functools.partial(gram_kernel, total_rows),
        grid=(parts,),
        out_shape=jax.ShapeDtypeStruct(packed, jnp.float32),
        in_specs=[pl.BlockSpec((count // parts, nx), lambda i: (i, 0))],
        out_specs=pl.BlockSpec(packed, lambda i: (0, 0)),
        scratch_shapes=[pltpu.VMEM((nx, nx), jnp.float32)] * 2,
        compiler_params=pltpu.CompilerParams(vmem_limit_bytes=VMEM_LIMIT),
        name="gram",
    )(rows)


def tree_sum(terms):
    while len(terms) > 1:
        terms = [a + b for a, b in zip(terms[::2], terms[1::2])]
    return terms[0]


def eliminate(block):
    size = block.shape[0]
    groups = size // 8
    row8 = lax.broadcasted_iota(jnp.int32, (8, size), 0)
    lane8 = lax.broadcasted_iota(jnp.int32, (8, size), 1)
    work = [block[8 * g : 8 * g + 8] for g in range(groups)]
    side = [jnp.where(row8 + 8 * g == lane8, 1.0, 0.0) for g in range(groups)]
    for p in range(groups):
        rows, arows = work[p], side[p]
        spread = [jnp.broadcast_to(rows[:, 8 * p + m : 8 * p + m + 1], (8, size)) for m in range(8)]
        unit, aunit = [], []
        for m in range(8):
            inv = 1.0 / jnp.broadcast_to(spread[m][m : m + 1], (8, size))
            unit.append(jnp.broadcast_to(rows[m : m + 1], (8, size)) * inv)
            aunit.append(jnp.broadcast_to(arows[m : m + 1], (8, size)) * inv)
            if m < 7:
                mult = jnp.where(row8 > m, spread[m], 0.0)
                rows = rows - mult * unit[m]
                arows = arows - mult * aunit[m]
                for t in range(m + 1, 8):
                    spread[t] = spread[t] - mult * (jnp.broadcast_to(spread[t][m : m + 1], (8, size)) * inv)
        work[p], side[p] = rows, arows
        if p + 1 < groups:
            tall = rows.T
            for q in range(p + 1, groups):
                mults = [jnp.broadcast_to(tall[8 * q : 8 * q + 8, m : m + 1], (8, size)) for m in range(8)]
                work[q] = work[q] - tree_sum([a * b for a, b in zip(mults, unit)])
                side[q] = side[q] - tree_sum([a * b for a, b in zip(mults, aunit)])
    return jnp.concatenate(work, axis=0), jnp.concatenate(side, axis=0)


def factor_kernel(gram_ref, factor_ref, inv_ref, work, side):
    n = factor_ref.shape[0]
    step = STEP
    count = n // step
    big = (((1,), (0,)), ((), ()))
    tall = (((0,), (0,)), ((), ()))
    rows = lax.broadcasted_iota(jnp.int32, (step, step), 0)
    cols = lax.broadcasted_iota(jnp.int32, (step, step), 1)
    col_n = lax.broadcasted_iota(jnp.int32, (step, n), 1)
    row_n = lax.broadcasted_iota(jnp.int32, (step, n), 0)
    work[...] = jnp.zeros_like(work)
    for b, (i, j) in enumerate(upper_blocks(n)):
        work[i * step : (i + 1) * step, j * step : (j + 1) * step] = gram_ref[b * step : (b + 1) * step, :]
    side[...] = jnp.zeros_like(side)

    def block_step(k, carry):
        lo = pl.multiple_of(k * step, step)
        here = pl.ds(lo, step)
        upper, lower = eliminate(work[here, here])
        pivot = jnp.sum(jnp.where(rows == cols, upper, 0.0), axis=1, keepdims=True)
        scale = 1.0 / jnp.sqrt(pivot)
        linv = lower * scale
        solved = lax.dot_general(linv, work[here, :], big, precision=HIGHEST, preferred_element_type=jnp.float32)
        factor_ref[here, :] = jnp.where(col_n >= row_n + lo, solved, 0.0)
        factor_ref[here, here] = jnp.where(cols >= rows, upper * scale, 0.0)
        left = side[here, :]
        left = lax.dot_general(linv, left, big, precision=HIGHEST, preferred_element_type=jnp.float32)
        inv_ref[here, :] = left
        inv_ref[here, here] = linv

        def trail(i, c):
            there = pl.ds(pl.multiple_of(i * step, step), step)
            mult = factor_ref[here, there]
            work[there, :] -= lax.dot_general(mult, factor_ref[here, :], tall, precision=HIGHEST, preferred_element_type=jnp.float32)
            side[there, :] -= lax.dot_general(mult, inv_ref[here, :], tall, precision=HIGHEST, preferred_element_type=jnp.float32)
            return c

        lax.fori_loop(k + 1, count, trail, 0)
        return carry

    lax.fori_loop(0, count, block_step, 0)


def factor_call(gram, n):
    shape = jax.ShapeDtypeStruct((n, n), jnp.float32)
    return pl.pallas_call(
        factor_kernel,
        out_shape=[shape, shape],
        in_specs=[pl.BlockSpec(memory_space=pltpu.VMEM)],
        out_specs=[pl.BlockSpec(memory_space=pltpu.VMEM)] * 2,
        scratch_shapes=[pltpu.VMEM((n, n), jnp.float32)] * 2,
        compiler_params=pltpu.CompilerParams(vmem_limit_bytes=VMEM_LIMIT),
        name="factor",
    )(gram)


FAST = 2


def sum_kernel(nby, nbz, in_ref, out_ref, land_a, land_b, part, send_a, recv_a, send_b, recv_b, send_c, recv_c, send_d, recv_d):
    na, nb = nby * FAST, nbz // FAST
    rows_a = in_ref.shape[0] // na
    rows_b = rows_a // nb
    by, bz = lax.axis_index("by"), lax.axis_index("bz")
    a = by * FAST + bz % FAST
    z = bz // FAST

    def plane_peer(d):
        t = (a + d) % na
        return t, (t // FAST, z * FAST + t % FAST)

    def line_peer(d):
        t = (z + d) % nb
        return t, (by, t * FAST + bz % FAST)

    barrier = pltpu.get_barrier_semaphore()
    for d in range(1, na):
        pl.semaphore_signal(barrier, inc=1, device_id=plane_peer(d)[1], device_id_type=pl.DeviceIdType.MESH)
    for d in range(1, nb):
        pl.semaphore_signal(barrier, inc=1, device_id=line_peer(d)[1], device_id_type=pl.DeviceIdType.MESH)
    pl.semaphore_wait(barrier, na + nb - 2)

    def exchange(peer, count, send, recv, source, target):
        copies = []
        for d in range(1, count):
            t, where = peer(d)
            copy = pltpu.make_async_remote_copy(
                src_ref=source(t),
                dst_ref=target(d),
                send_sem=send.at[d - 1],
                recv_sem=recv.at[d - 1],
                device_id=where,
                device_id_type=pl.DeviceIdType.MESH,
            )
            copy.start()
            copies.append(copy)
        for copy in copies:
            copy.wait()

    def rows_at(base, size):
        return pl.ds(pl.multiple_of(base, 8), size)

    exchange(plane_peer, na, send_a, recv_a, lambda t: in_ref.at[rows_at(t * rows_a, rows_a)], lambda d: land_a.at[d - 1])
    part[...] = in_ref[rows_at(a * rows_a, rows_a), :] + tree_any([land_a[d] for d in range(na - 1)])
    exchange(line_peer, nb, send_b, recv_b, lambda t: part.at[rows_at(t * rows_b, rows_b)], lambda d: land_b.at[d - 1])
    mine = rows_at(a * rows_a + z * rows_b, rows_b)
    out_ref[mine, :] = part[rows_at(z * rows_b, rows_b), :] + tree_any([land_b[d] for d in range(nb - 1)])
    exchange(line_peer, nb, send_c, recv_c, lambda t: out_ref.at[mine], lambda d: out_ref.at[mine])
    ours = rows_at(a * rows_a, rows_a)
    exchange(plane_peer, na, send_d, recv_d, lambda t: out_ref.at[ours], lambda d: out_ref.at[ours])


def tree_any(terms):
    total = terms[0]
    for term in terms[1:]:
        total = total + term
    return total


def sum_call(packed):
    nby, nbz = lax.axis_size("by"), lax.axis_size("bz")
    na, nb = nby * FAST, nbz // FAST
    rows, cols = packed.shape
    if nbz % FAST or nb < 2 or rows % (8 * na * nb):
        return lax.psum(packed, ("by", "bz"))
    rows_a = rows // na
    rows_b = rows_a // nb
    sems = [pltpu.SemaphoreType.DMA((c - 1,)) for c in (na, na, nb, nb, nb, nb, na, na)]
    return pl.pallas_call(
        functools.partial(sum_kernel, nby, nbz),
        out_shape=jax.ShapeDtypeStruct(packed.shape, jnp.float32),
        in_specs=[pl.BlockSpec(memory_space=pltpu.VMEM)],
        out_specs=pl.BlockSpec(memory_space=pltpu.VMEM),
        scratch_shapes=[
            pltpu.VMEM((na - 1, rows_a, cols), jnp.float32),
            pltpu.VMEM((nb - 1, rows_b, cols), jnp.float32),
            pltpu.VMEM((rows_a, cols), jnp.float32),
            *sems,
        ],
        compiler_params=pltpu.CompilerParams(collective_id=0, has_side_effects=True, vmem_limit_bytes=VMEM_LIMIT),
        name="sum_all",
    )(packed)


def on_device(fields, conductance):
    nf, ny, nz, nx = fields.shape
    total_rows = nf * ny * lax.axis_size("by") * nz * lax.axis_size("bz")
    relaxed = relax_call(fields, conductance)
    rows = relaxed.reshape(-1, nx)
    packed = gram_call(rows, total_rows, nf)
    factor, linv = factor_call(sum_call(packed), nx)
    basis = lax.dot_general(
        rows, linv, (((1,), (1,)), ((), ())), precision=HIGH, preferred_element_type=jnp.float32
    )
    return (basis.reshape(relaxed.shape), factor)


def solution(mesh):
    return jax.shard_map(
        on_device,
        mesh=mesh,
        in_specs=(P(None, "by", "bz", None), P("by", "bz", None)),
        out_specs=(P(None, "by", "bz", None), P()),
        check_vma=False,
    )
```

```python
import functools

import jax
import jax.numpy as jnp
from jax import lax
from jax.experimental import pallas as pl
from jax.experimental.pallas import tpu as pltpu
from jax.sharding import PartitionSpec as P

VMEM_LIMIT = 58 * 1024 * 1024
HIGHEST = lax.Precision.HIGHEST
HIGH = lax.Precision.HIGH
STEP = 128


def upper_blocks(n):
    count = n // STEP
    return [(i, j) for i in range(count) for j in range(i, count)]


def strip(src, root, store, y, z, nf, nx, lane):
    plain = root[y + 1, pl.ds(8 + z, 8), :]
    centre = 0.125 * plain
    wyp = centre * root[y + 2, pl.ds(8 + z, 8), :]
    wym = centre * root[y, pl.ds(8 + z, 8), :]
    wzp = centre * root[y + 1, pl.ds(9 + z, 8), :]
    wzm = centre * root[y + 1, pl.ds(7 + z, 8), :]
    wxp = jnp.where(lane == nx - 1, 0.0, centre * pltpu.roll(plain, nx - 1, 1))
    wxm = jnp.where(lane == 0, 0.0, centre * pltpu.roll(plain, 1, 1))
    keep = 1.0 - (((wyp + wym) + (wzp + wzm)) + (wxp + wxm))
    for f in range(nf):
        mid = src[f, y + 1, pl.ds(8 + z, 8), :]
        near = wyp * src[f, y + 2, pl.ds(8 + z, 8), :] + wym * src[f, y, pl.ds(8 + z, 8), :]
        side = wzp * src[f, y + 1, pl.ds(9 + z, 8), :] + wzm * src[f, y + 1, pl.ds(7 + z, 8), :]
        along = wxp * pltpu.roll(mid, nx - 1, 1) + wxm * pltpu.roll(mid, 1, 1)
        store(f, y, z, (keep * mid + near) + (side + along))


def relax_kernel(nby, nbz, u_ref, k_ref, out_ref, ext, again, root, kland, zsend, zland, zsend2, zland2, load_sem, send, recv):
    nf, ny, nz, nx = u_ref.shape
    top = 8 + nz
    by, bz = lax.axis_index("by"), lax.axis_index("bz")
    has = [by > 0, by < nby - 1, bz > 0, bz < nbz - 1]
    peer = [(by - 1, bz), (by + 1, bz), (by, bz - 1), (by, bz + 1)]
    inner = pl.ds(8, nz)
    halo = [0, ny + 1]
    mesh_id = pl.DeviceIdType.MESH

    load = pltpu.make_async_copy(u_ref, ext.at[:, pl.ds(1, ny), inner, :], load_sem)
    load.start()

    def send_item(d, base, src, place):
        return pltpu.make_async_remote_copy(
            src_ref=src,
            dst_ref=place((d + 1) % 2),
            send_sem=send.at[base + d % 2],
            recv_sem=recv.at[base + (d + 1) % 2],
            device_id=peer[d],
            device_id_type=mesh_id,
        )

    def recv_item(d, base, src, place):
        return pltpu.make_async_remote_copy(
            src_ref=src,
            dst_ref=place(d % 2),
            send_sem=send.at[base + d % 2],
            recv_sem=recv.at[base + d % 2],
            device_id=peer[d],
            device_id_type=mesh_id,
        )

    def start(items):
        for d, base, src, place in items:
            @pl.when(has[d])
            def _(d=d, base=base, src=src, place=place):
                send_item(d, base, src, place).start()

    def finish(items):
        for d, base, src, place in items:
            @pl.when(has[d])
            def _(d=d, base=base, src=src, place=place):
                recv_item(d, base, src, place).wait_recv()
                send_item(d, base, src, place).wait_send()

    barrier = pltpu.get_barrier_semaphore()
    for d in range(4):
        @pl.when(has[d])
        def _(d=d):
            pl.semaphore_signal(barrier, inc=1, device_id=peer[d], device_id_type=mesh_id)
    pl.semaphore_wait(barrier, sum(jnp.where(h, 1, 0) for h in has))

    ends = [0, ny - 1]
    first_y = [(d, 0, u_ref.at[:, ends[d]], lambda s: ext.at[:, halo[s], inner, :]) for d in range(2)]
    first_k = [(d, 2, k_ref.at[ends[d]], lambda s: kland.at[s]) for d in range(2)]
    start(first_y + first_k)

    for d in range(2):
        @pl.when(jnp.logical_not(has[d]))
        def _(d=d):
            for f in range(nf):
                ext[f, halo[d], inner, :] = jnp.zeros((nz, nx), jnp.float32)
                again[f, halo[d], inner, :] = jnp.zeros((nz, nx), jnp.float32)
            kland[d] = jnp.zeros((nz, nx), jnp.float32)

        @pl.when(jnp.logical_not(has[d + 2]))
        def _(d=d):
            zland[d] = jnp.zeros(zland.shape[1:], jnp.float32)
            zland2[d] = jnp.zeros(zland2.shape[1:], jnp.float32)

    zsend[0, nf] = k_ref[:, 0, :]
    zsend[1, nf] = k_ref[:, nz - 1, :]
    load.wait()
    for f in range(nf):
        zsend[0, f] = ext[f, pl.ds(1, ny), 8, :]
        zsend[1, f] = ext[f, pl.ds(1, ny), top - 1, :]
    first_z = [(d, 4, zsend.at[d - 2], lambda s: zland.at[s]) for d in (2, 3)]
    start(first_z)

    def fill_root(y, carry):
        root[y + 1, inner, :] = jnp.sqrt(k_ref[y])
        return carry

    lax.fori_loop(0, ny, fill_root, 0)
    lane = lax.broadcasted_iota(jnp.int32, (8, nx), 1)

    def to_again(f, y, z, value):
        again[f, y + 1, pl.ds(8 + z, 8), :] = value

    def to_out(f, y, z, value):
        out_ref[f, y, pl.ds(z, 8), :] = value

    def inside(src, store):
        def body(y, carry):
            for z in range(8, nz - 8, 8):
                strip(src, root, store, y, z, nf, nx, lane)
            return carry

        lax.fori_loop(1, ny - 1, body, 0)

    def border(src, store):
        def planes(i, carry):
            for z in range(0, nz, 8):
                strip(src, root, store, i * (ny - 1), z, nf, nx, lane)
            return carry

        def strips(y, carry):
            for z in (0, nz - 8):
                strip(src, root, store, y, z, nf, nx, lane)
            return carry

        lax.fori_loop(0, 2, planes, 0)
        lax.fori_loop(1, ny - 1, strips, 0)

    inside(ext, to_again)
    finish(first_y + first_k + first_z)
    for d, row in ((0, 7), (1, top)):
        root[halo[d], inner, :] = jnp.sqrt(kland[d])
        root[pl.ds(1, ny), row : row + 1, :] = jnp.sqrt(zland[d, nf])[:, None, :]
        for f in range(nf):
            ext[f, pl.ds(1, ny), row : row + 1, :] = zland[d, f][:, None, :]
    border(ext, to_again)

    for f in range(nf):
        zsend2[0, f] = again[f, pl.ds(1, ny), 8, :]
        zsend2[1, f] = again[f, pl.ds(1, ny), top - 1, :]
    second = [(d, 6, again.at[:, ends[d] + 1, inner, :], lambda s: again.at[:, halo[s], inner, :]) for d in range(2)]
    second += [(d, 8, zsend2.at[d - 2], lambda s: zland2.at[s]) for d in (2, 3)]
    start(second)
    inside(again, to_out)
    finish(second)
    for d, row in ((0, 7), (1, top)):
        for f in range(nf):
            again[f, pl.ds(1, ny), row : row + 1, :] = zland2[d, f][:, None, :]
    border(again, to_out)


def relax_call(u, k):
    nf, ny, nz, nx = u.shape
    cells = pltpu.VMEM((nf, ny + 2, nz + 16, nx), jnp.float32)
    return pl.pallas_call(
        functools.partial(relax_kernel, lax.axis_size("by"), lax.axis_size("bz")),
        out_shape=jax.ShapeDtypeStruct(u.shape, jnp.float32),
        in_specs=[pl.BlockSpec(memory_space=pl.ANY), pl.BlockSpec(memory_space=pltpu.VMEM)],
        out_specs=pl.BlockSpec(memory_space=pltpu.VMEM),
        scratch_shapes=[
            cells,
            cells,
            pltpu.VMEM((ny + 2, nz + 16, nx), jnp.float32),
            pltpu.VMEM((2, nz, nx), jnp.float32),
            pltpu.VMEM((2, nf + 1, ny, nx), jnp.float32),
            pltpu.VMEM((2, nf + 1, ny, nx), jnp.float32),
            pltpu.VMEM((2, nf, ny, nx), jnp.float32),
            pltpu.VMEM((2, nf, ny, nx), jnp.float32),
            pltpu.SemaphoreType.DMA,
            pltpu.SemaphoreType.DMA((10,)),
            pltpu.SemaphoreType.DMA((10,)),
        ],
        compiler_params=pltpu.CompilerParams(collective_id=1, has_side_effects=True, vmem_limit_bytes=VMEM_LIMIT),
        name="relax",
    )(u, k)


def gram_kernel(total_rows, rows_ref, gram_ref, head, cross):
    nx = rows_ref.shape[1]
    half = nx // 2
    tall = (((0,), (0,)), ((), ()))
    step = pl.program_id(0)

    @pl.when(step == 0)
    def _():
        head[...] = jnp.zeros_like(head)
        cross[...] = jnp.zeros_like(cross)

    x = rows_ref[...]
    hi = x.astype(jnp.bfloat16)
    lo = (x - hi.astype(jnp.float32)).astype(jnp.bfloat16)
    for c in range(2):
        cols = slice(c * half, (c + 1) * half)
        left = hi[:, cols]
        cross[cols, :] += lax.dot_general(left, lo, tall, preferred_element_type=jnp.float32)
        head[cols, c * half :] += lax.dot_general(left, hi[:, c * half :], tall, preferred_element_type=jnp.float32)

    @pl.when(step == pl.num_programs(0) - 1)
    def _():
        for b, (i, j) in enumerate(upper_blocks(nx)):
            ri, rj = slice(i * STEP, (i + 1) * STEP), slice(j * STEP, (j + 1) * STEP)
            total = head[ri, rj] + (cross[ri, rj] + cross[rj, ri].T)
            gram_ref[b * STEP : (b + 1) * STEP, :] = total / jnp.float32(total_rows)


def gram_call(rows, total_rows, parts):
    count, nx = rows.shape
    packed = (len(upper_blocks(nx)) * STEP, STEP)
    return pl.pallas_call(
        functools.partial(gram_kernel, total_rows),
        grid=(parts,),
        out_shape=jax.ShapeDtypeStruct(packed, jnp.float32),
        in_specs=[pl.BlockSpec((count // parts, nx), lambda i: (i, 0))],
        out_specs=pl.BlockSpec(packed, lambda i: (0, 0)),
        scratch_shapes=[pltpu.VMEM((nx, nx), jnp.float32)] * 2,
        compiler_params=pltpu.CompilerParams(vmem_limit_bytes=VMEM_LIMIT),
        name="gram",
    )(rows)


def tree_sum(terms):
    while len(terms) > 1:
        terms = [a + b for a, b in zip(terms[::2], terms[1::2])]
    return terms[0]


def eliminate(block):
    size = block.shape[0]
    groups = size // 8
    row8 = lax.broadcasted_iota(jnp.int32, (8, size), 0)
    lane8 = lax.broadcasted_iota(jnp.int32, (8, size), 1)
    work = [block[8 * g : 8 * g + 8] for g in range(groups)]
    side = [jnp.where(row8 + 8 * g == lane8, 1.0, 0.0) for g in range(groups)]
    for p in range(groups):
        rows, arows = work[p], side[p]
        spread = [jnp.broadcast_to(rows[:, 8 * p + m : 8 * p + m + 1], (8, size)) for m in range(8)]
        unit, aunit = [], []
        for m in range(8):
            inv = 1.0 / jnp.broadcast_to(spread[m][m : m + 1], (8, size))
            unit.append(jnp.broadcast_to(rows[m : m + 1], (8, size)) * inv)
            aunit.append(jnp.broadcast_to(arows[m : m + 1], (8, size)) * inv)
            if m < 7:
                mult = jnp.where(row8 > m, spread[m], 0.0)
                rows = rows - mult * unit[m]
                arows = arows - mult * aunit[m]
                for t in range(m + 1, 8):
                    spread[t] = spread[t] - mult * (jnp.broadcast_to(spread[t][m : m + 1], (8, size)) * inv)
        work[p], side[p] = rows, arows
        if p + 1 < groups:
            tall = rows.T
            for q in range(p + 1, groups):
                mults = [jnp.broadcast_to(tall[8 * q : 8 * q + 8, m : m + 1], (8, size)) for m in range(8)]
                work[q] = work[q] - tree_sum([a * b for a, b in zip(mults, unit)])
                side[q] = side[q] - tree_sum([a * b for a, b in zip(mults, aunit)])
    return jnp.concatenate(work, axis=0), jnp.concatenate(side, axis=0)


def factor_kernel(gram_ref, factor_ref, inv_ref, work, side):
    n = factor_ref.shape[0]
    step = STEP
    count = n // step
    big = (((1,), (0,)), ((), ()))
    tall = (((0,), (0,)), ((), ()))
    rows = lax.broadcasted_iota(jnp.int32, (step, step), 0)
    cols = lax.broadcasted_iota(jnp.int32, (step, step), 1)
    col_n = lax.broadcasted_iota(jnp.int32, (step, n), 1)
    row_n = lax.broadcasted_iota(jnp.int32, (step, n), 0)
    work[...] = jnp.zeros_like(work)
    for b, (i, j) in enumerate(upper_blocks(n)):
        work[i * step : (i + 1) * step, j * step : (j + 1) * step] = gram_ref[b * step : (b + 1) * step, :]
    side[...] = jnp.zeros_like(side)

    def block_step(k, carry):
        lo = pl.multiple_of(k * step, step)
        here = pl.ds(lo, step)
        upper, lower = eliminate(work[here, here])
        pivot = jnp.sum(jnp.where(rows == cols, upper, 0.0), axis=1, keepdims=True)
        scale = 1.0 / jnp.sqrt(pivot)
        linv = lower * scale
        solved = lax.dot_general(linv, work[here, :], big, precision=HIGHEST, preferred_element_type=jnp.float32)
        factor_ref[here, :] = jnp.where(col_n >= row_n + lo, solved, 0.0)
        factor_ref[here, here] = jnp.where(cols >= rows, upper * scale, 0.0)
        left = side[here, :]
        left = lax.dot_general(linv, left, big, precision=HIGHEST, preferred_element_type=jnp.float32)
        inv_ref[here, :] = left
        inv_ref[here, here] = linv

        def trail(i, c):
            there = pl.ds(pl.multiple_of(i * step, step), step)
            mult = factor_ref[here, there]
            work[there, :] -= lax.dot_general(mult, factor_ref[here, :], tall, precision=HIGHEST, preferred_element_type=jnp.float32)
            side[there, :] -= lax.dot_general(mult, inv_ref[here, :], tall, precision=HIGHEST, preferred_element_type=jnp.float32)
            return c

        lax.fori_loop(k + 1, count, trail, 0)
        return carry

    lax.fori_loop(0, count, block_step, 0)


def factor_call(gram, n):
    shape = jax.ShapeDtypeStruct((n, n), jnp.float32)
    return pl.pallas_call(
        factor_kernel,
        out_shape=[shape, shape],
        in_specs=[pl.BlockSpec(memory_space=pltpu.VMEM)],
        out_specs=[pl.BlockSpec(memory_space=pltpu.VMEM)] * 2,
        scratch_shapes=[pltpu.VMEM((n, n), jnp.float32)] * 2,
        compiler_params=pltpu.CompilerParams(vmem_limit_bytes=VMEM_LIMIT),
        name="factor",
    )(gram)


FAST = 2


def sum_kernel(nby, nbz, in_ref, out_ref, land_a, land_b, part, send_a, recv_a, send_b, recv_b, send_c, recv_c, send_d, recv_d):
    na, nb = nby * FAST, nbz // FAST
    rows_a = in_ref.shape[0] // na
    rows_b = rows_a // nb
    by, bz = lax.axis_index("by"), lax.axis_index("bz")
    a = by * FAST + bz % FAST
    z = bz // FAST

    def plane_peer(d):
        t = (a + d) % na
        return t, (t // FAST, z * FAST + t % FAST)

    def line_peer(d):
        t = (z + d) % nb
        return t, (by, t * FAST + bz % FAST)

    barrier = pltpu.get_barrier_semaphore()
    for d in range(1, na):
        pl.semaphore_signal(barrier, inc=1, device_id=plane_peer(d)[1], device_id_type=pl.DeviceIdType.MESH)
    for d in range(1, nb):
        pl.semaphore_signal(barrier, inc=1, device_id=line_peer(d)[1], device_id_type=pl.DeviceIdType.MESH)
    pl.semaphore_wait(barrier, na + nb - 2)

    def exchange(peer, count, send, recv, source, target):
        copies = []
        for d in range(1, count):
            t, where = peer(d)
            copy = pltpu.make_async_remote_copy(
                src_ref=source(t),
                dst_ref=target(d),
                send_sem=send.at[d - 1],
                recv_sem=recv.at[d - 1],
                device_id=where,
                device_id_type=pl.DeviceIdType.MESH,
            )
            copy.start()
            copies.append(copy)
        for copy in copies:
            copy.wait()

    def rows_at(base, size):
        return pl.ds(pl.multiple_of(base, 8), size)

    exchange(plane_peer, na, send_a, recv_a, lambda t: in_ref.at[rows_at(t * rows_a, rows_a)], lambda d: land_a.at[d - 1])
    part[...] = in_ref[rows_at(a * rows_a, rows_a), :] + tree_any([land_a[d] for d in range(na - 1)])
    exchange(line_peer, nb, send_b, recv_b, lambda t: part.at[rows_at(t * rows_b, rows_b)], lambda d: land_b.at[d - 1])
    mine = rows_at(a * rows_a + z * rows_b, rows_b)
    out_ref[mine, :] = part[rows_at(z * rows_b, rows_b), :] + tree_any([land_b[d] for d in range(nb - 1)])
    exchange(line_peer, nb, send_c, recv_c, lambda t: out_ref.at[mine], lambda d: out_ref.at[mine])
    ours = rows_at(a * rows_a, rows_a)
    exchange(plane_peer, na, send_d, recv_d, lambda t: out_ref.at[ours], lambda d: out_ref.at[ours])


def tree_any(terms):
    total = terms[0]
    for term in terms[1:]:
        total = total + term
    return total


def sum_call(packed):
    nby, nbz = lax.axis_size("by"), lax.axis_size("bz")
    na, nb = nby * FAST, nbz // FAST
    rows, cols = packed.shape
    if nbz % FAST or nb < 2 or rows % (8 * na * nb):
        return lax.psum(packed, ("by", "bz"))
    rows_a = rows // na
    rows_b = rows_a // nb
    sems = [pltpu.SemaphoreType.DMA((c - 1,)) for c in (na, na, nb, nb, nb, nb, na, na)]
    return pl.pallas_call(
        functools.partial(sum_kernel, nby, nbz),
        out_shape=jax.ShapeDtypeStruct(packed.shape, jnp.float32),
        in_specs=[pl.BlockSpec(memory_space=pltpu.VMEM)],
        out_specs=pl.BlockSpec(memory_space=pltpu.VMEM),
        scratch_shapes=[
            pltpu.VMEM((na - 1, rows_a, cols), jnp.float32),
            pltpu.VMEM((nb - 1, rows_b, cols), jnp.float32),
            pltpu.VMEM((rows_a, cols), jnp.float32),
            *sems,
        ],
        compiler_params=pltpu.CompilerParams(collective_id=0, has_side_effects=True, vmem_limit_bytes=VMEM_LIMIT),
        name="sum_all",
    )(packed)


def on_device(fields, conductance):
    nf, ny, nz, nx = fields.shape
    total_rows = nf * ny * lax.axis_size("by") * nz * lax.axis_size("bz")
    relaxed = relax_call(fields, conductance)
    rows = relaxed.reshape(-1, nx)
    packed = gram_call(rows, total_rows, max(nf // 2, 1))
    factor, linv = factor_call(sum_call(packed), nx)
    basis = lax.dot_general(
        rows, linv, (((1,), (1,)), ((), ())), precision=HIGH, preferred_element_type=jnp.float32
    )
    return (basis.reshape(relaxed.shape), factor)


def solution(mesh):
    return jax.shard_map(
        on_device,
        mesh=mesh,
        in_specs=(P(None, "by", "bz", None), P("by", "bz", None)),
        out_specs=(P(None, "by", "bz", None), P()),
        check_vma=False,
    )
```
